32 devices in a mesh: seq: 16 (over z, y, core), head: 2 (over x).
Axes of the slice: x: 2, y: 2, z: 4, core: 2. Of those that a mesh axis runs over, the one named last changes fastest.
Arguments:
- queries: bfloat16 [2048, 6144], P('seq', 'head'), may hold values from -5 to 5
- key_rows: bfloat16 [2048, 6144], P('seq', 'head'), may hold values from -5 to 5
- value_rows: bfloat16 [2048, 6144], P('seq', 'head'), may hold values from -6 to 6
- out_grad: bfloat16 [2048, 6144], P('seq', 'head'), may hold values from -6 to 6
- partner: int32 [32, 48, 2], P('seq', 'head'), may hold values from 0 to 31, as said below
Outputs:
- query_gradient: bfloat16 [2048, 6144], P(('seq', 'head'))
- key_grad: bfloat16 [2048, 6144], P(('seq', 'head'))
- value_grad: bfloat16 [2048, 6144], P(('seq', 'head'))
The draws below stay inside these ranges and needn't reach their ends.
Inputs may be any that keep to these rules, and one draw needn't show every extreme that they name: `partner`: each entry is o * 2 + j for an owner o of the seq axis and a block j of it. Among the 96 entries of the rows of one device (its query blocks and its heads), at most 9 have the same owner; in every draw one owner, the same for all devices of one index of head, gets exactly 9 entries from each of them.
All inputs are finite; a program needn't handle non-finite values.
Results may differ from the reference program's by a relative error of at most 0.012.
Values may be sent and summed in bfloat16 or wider, within the bound.
A program may use at most 128 MiB of HBM per device.

```python
import math
import jax
import jax.numpy as jnp
from jax import lax

HEADS = 48
DH = 128
BLOCK = 64
RAND = 2
BLK_DEV = 2
HEADS_DEV = 24
TOKENS = 2048
NB = 32
CAP = 9


def normal_rows(key, salt):
    draws = jax.random.normal(jax.random.fold_in(key, salt), (TOKENS, HEADS * DH), jnp.float32)
    return jnp.clip(draws, -4.5, 4.5)


def draw_queries(key, part):
    normal = normal_rows(key, 1)
    return normal.astype(jnp.bfloat16)


def draw_key_rows(key, part):
    normal = normal_rows(key, 2)
    return normal.astype(jnp.bfloat16)


def draw_partner(key, part):
    owner_count = NB // BLK_DEV
    head_groups = HEADS // HEADS_DEV
    request_count = RAND * BLK_DEV * HEADS_DEV
    owner_pool = jnp.tile(jnp.arange(owner_count, dtype=jnp.int32), CAP)
    hot_owners = jax.random.randint(jax.random.fold_in(key, 7), (head_groups,), 0, owner_count, dtype=jnp.int32)

    def one_device(device_key, hot_owner):
        shuffled = jax.random.permutation(jax.random.fold_in(device_key, 1), owner_pool)
        sort_score = jnp.where(shuffled == hot_owner, 0, 1 + jnp.arange(owner_pool.shape[0], dtype=jnp.int32))
        ranking = jnp.argsort(sort_score, stable=True)
        chosen = shuffled[ranking][:request_count]
        chosen = jax.random.permutation(jax.random.fold_in(device_key, 2), chosen)
        local_blocks = jax.random.randint(jax.random.fold_in(device_key, 3), (request_count,), 0, BLK_DEV, dtype=jnp.int32)
        return chosen * BLK_DEV + local_blocks
    device_keys = jax.random.split(jax.random.fold_in(key, 9), owner_count * head_groups)
    hot_each = jnp.tile(hot_owners, owner_count)
    partner_table = jax.vmap(one_device)(device_keys, hot_each)
    partner_table = partner_table.reshape(owner_count, head_groups, BLK_DEV, HEADS_DEV, RAND).transpose(0, 2, 1, 3, 4)
    return partner_table.reshape(NB, HEADS, RAND).astype(jnp.int32)


def shard_levels(stream_key, shape, cuts, least, high):
    factor_of = 1.0
    for dim, shards_of in cuts:
        heights = jax.random.uniform(jax.random.fold_in(jax.random.fold_in(stream_key, 6), dim), (shards_of,), jnp.float32, least / len(cuts), high / len(cuts))
        factor_of = factor_of * jnp.repeat(jnp.exp(heights), shape[dim] // shards_of).reshape((-1,) + (1,) * (len(shape) - 1 - dim))
    return factor_of


def centred(rng, extent, deviation, limit, pieces=(), kind=jnp.bfloat16):
    values = jax.random.normal(rng, extent, jnp.float32) * deviation
    if len(pieces) > 0:
        values = shard_levels(rng, extent, pieces, -0.22, 0.18) * values
    return jnp.clip(values, min=-limit, max=limit).astype(kind)


def setup_inputs(seed: int = 0) -> dict:
    key_of = jax.random.split(jax.random.key(seed), 6)
    queries = draw_queries(jax.random.fold_in(key_of[5], 71), 0)
    key_rows = draw_key_rows(jax.random.fold_in(key_of[5], 71), 0)
    value_rows = centred(key_of[2], (TOKENS, HEADS * DH), 1.0, 6.0, ((0, 16), (1, 2)))
    out_grad = centred(key_of[3], (TOKENS, HEADS * DH), 1.0, 6.0, ((0, 16), (1, 2)))
    partner = draw_partner(jax.random.fold_in(key_of[5], 71), 0)
    return {"queries": queries, "key_rows": key_rows, "value_rows": value_rows, "out_grad": out_grad, "partner": partner}


def gather_blocks(contrib, partner_head):
    block_count = contrib.shape[0]
    window_part = contrib[:, :3 * BLOCK].reshape(block_count, 3, BLOCK, DH)
    zero_block = jnp.zeros((1, BLOCK, DH), jnp.float32)
    summed = window_part[:, 1]
    summed = summed + jnp.concatenate([window_part[1:, 0], zero_block], axis=0)
    summed = summed + jnp.concatenate([zero_block, window_part[:-1, 2]], axis=0)
    random_part = contrib[:, 3 * BLOCK:].reshape(block_count * RAND, BLOCK, DH)
    summed = summed + jax.ops.segment_sum(random_part, partner_head.reshape(block_count * RAND), num_segments=block_count)
    return summed

def head_grads(operands):
    query_head, key_head, value_head, grad_head, partner_head = operands
    block_count = query_head.shape[0]
    similarity_multiplier = 1.0 / math.sqrt(DH)
    zero_block = jnp.zeros((1, BLOCK, DH), key_head.dtype)
    padded_keys = jnp.concatenate([zero_block, key_head, zero_block], axis=0)
    padded_values = jnp.concatenate([zero_block, value_head, zero_block], axis=0)
    window_keys = jnp.concatenate([padded_keys[:-2], padded_keys[1:-1], padded_keys[2:]], axis=1)
    window_values = jnp.concatenate([padded_values[:-2], padded_values[1:-1], padded_values[2:]], axis=1)
    random_keys = key_head[partner_head].reshape(block_count, RAND * BLOCK, DH)
    random_values = value_head[partner_head].reshape(block_count, RAND * BLOCK, DH)
    combined_keys = jnp.concatenate([window_keys, random_keys], axis=1).astype(jnp.float32)
    combined_values = jnp.concatenate([window_values, random_values], axis=1).astype(jnp.float32)
    block_ids = jnp.arange(block_count)
    filled = jnp.ones((block_count, BLOCK), jnp.bool_)
    allowed = jnp.concatenate([filled & (block_ids > 0)[:, None], filled, filled & (block_ids < block_count - 1)[:, None], jnp.ones((block_count, RAND * BLOCK), jnp.bool_)], axis=1)
    probe_vector_for_one_row = query_head.astype(jnp.float32)
    derivative_for_one_row = grad_head.astype(jnp.float32)
    logit_scores = similarity_multiplier * jnp.einsum('rch,rsh->rcs', probe_vector_for_one_row, combined_keys)
    logit_scores = jnp.where(allowed[:, None, :], logit_scores, -jnp.inf)
    row_max = lax.optimization_barrier(jnp.max(logit_scores, axis=2, keepdims=True))
    log_total = row_max + jnp.log(lax.optimization_barrier(jnp.sum(jnp.exp(logit_scores - row_max), axis=2, keepdims=True)))
    weights = jnp.exp(logit_scores - log_total)
    reduced_precision_probabilities = lax.optimization_barrier(weights.astype(jnp.bfloat16)).astype(jnp.float32)
    attended_output = jnp.einsum('rzh,rhs->rzs', reduced_precision_probabilities, combined_values)
    attended_output = lax.optimization_barrier(attended_output.astype(jnp.bfloat16)).astype(jnp.float32)
    row_delta = lax.optimization_barrier(jnp.sum(derivative_for_one_row * attended_output, axis=2, keepdims=True))
    weight_gradient = jnp.einsum('rch,rsh->rcs', derivative_for_one_row, combined_values)
    similarity_derivative = lax.optimization_barrier((weights * (weight_gradient - row_delta)).astype(jnp.bfloat16)).astype(jnp.float32)
    query_gradient = similarity_multiplier * jnp.einsum('rzh,rhs->rzs', similarity_derivative, combined_keys)
    matching_vector_share = similarity_multiplier * jnp.einsum('oyb,oyj->obj', similarity_derivative, probe_vector_for_one_row)
    payload_vector_share = jnp.einsum('oyb,oyj->obj', reduced_precision_probabilities, derivative_for_one_row)
    key_grad = gather_blocks(matching_vector_share, partner_head)
    value_grad = gather_blocks(payload_vector_share, partner_head)
    return (query_gradient.astype(jnp.bfloat16), key_grad.astype(jnp.bfloat16), value_grad.astype(jnp.bfloat16))

def reference(queries, key_rows, value_rows, out_grad, partner):

    def by_head(matrix):
        return matrix.reshape(NB, BLOCK, HEADS, DH).transpose(2, 0, 1, 3)
    query_gradient, key_grad, value_grad = lax.map(head_grads, (by_head(queries), by_head(key_rows), by_head(value_rows), by_head(out_grad), partner.transpose(1, 0, 2)))

    def as_rows(grads):
        return grads.transpose(1, 2, 0, 3).reshape(TOKENS, HEADS * DH)
    return (as_rows(query_gradient), as_rows(key_grad), as_rows(value_grad))
```

```python
import functools
import math

import jax
import jax.numpy as jnp
from jax import lax
from jax.experimental import pallas as pl
from jax.experimental.pallas import tpu as pltpu
from jax.sharding import PartitionSpec as P

F32 = jnp.float32
BF16 = jnp.bfloat16
VMEM = pltpu.VMEM
LIMIT = 48 * 1024 * 1024


def dot(a, b, ca, cb):
    return lax.dot_general(a, b, (((ca,), (cb,)), ((), ())), preferred_element_type=F32)


def gather_kernel(block, dim, heads, cap, codes, k_ref, v_ref, o_ref):
    peer = pl.program_id(0)
    for j in range(cap):
        code = jnp.maximum(codes[peer * cap + j], 0)
        rows = pl.ds(pl.multiple_of(code // heads * block, block), block)
        cols = pl.ds(pl.multiple_of(code % heads * dim, dim), dim)
        o_ref[j, :, :dim] = k_ref[rows, cols]
        o_ref[j, :, dim:] = v_ref[rows, cols]


def attend_kernel(
    blocks, block, dim, heads, rand, step, scale,
    slots, edge, q_ref, k_ref, v_ref, g_ref, up_ref, down_ref, far_ref,
    dq_ref, dk_ref, dv_ref, tok_ref, tov_ref, tnk_ref, tnv_ref, out_ref,
):
    group = pl.program_id(0)
    for j in range(step):
        head = group * step + j
        cols = slice(j * dim, (j + 1) * dim)
        ks = [up_ref[0, :, cols]] + [k_ref[b * block:(b + 1) * block, cols] for b in range(blocks)]
        ks.append(down_ref[0, :, cols])
        vs = [up_ref[1, :, cols]] + [v_ref[b * block:(b + 1) * block, cols] for b in range(blocks)]
        vs.append(down_ref[1, :, cols])
        gk = [None] * (blocks + 2)
        gv = [None] * (blocks + 2)
        for b in range(blocks):
            rows = slice(b * block, (b + 1) * block)
            q = q_ref[rows, cols]
            g = g_ref[rows, cols]
            at = [slots[(b * heads + head) * rand + r] for r in range(rand)]
            keys = jnp.concatenate(ks[b:b + 3] + [far_ref[s, :, :dim] for s in at], axis=0)
            vals = jnp.concatenate(vs[b:b + 3] + [far_ref[s, :, dim:] for s in at], axis=0)
            s = scale * dot(q, keys, 1, 1)
            place = lax.broadcasted_iota(jnp.int32, s.shape, 1)
            if b == 0:
                s = jnp.where((place < block) & (edge[0] == 0), -jnp.inf, s)
            if b == blocks - 1:
                s = jnp.where(
                    (place >= 2 * block) & (place < 3 * block) & (edge[1] == 0), -jnp.inf, s
                )
            top = jnp.max(s, axis=1, keepdims=True)
            e = jnp.exp(s - top)
            w = e * (1.0 / jnp.sum(e, axis=1, keepdims=True))
            p = w.astype(BF16)
            o = dot(p, vals, 1, 0).astype(BF16).astype(F32)
            delta = jnp.sum(o * g.astype(F32), axis=1, keepdims=True)
            ds = (w * (dot(g, vals, 1, 1) - delta)).astype(BF16)
            dq_ref[rows, cols] = (scale * dot(ds, keys, 1, 0)).astype(BF16)
            dk = scale * dot(ds, q, 0, 0)
            dv = dot(p, g, 0, 0)
            for i in range(3):
                part = slice(i * block, (i + 1) * block)
                gk[b + i] = dk[part] if gk[b + i] is None else gk[b + i] + dk[part]
                gv[b + i] = dv[part] if gv[b + i] is None else gv[b + i] + dv[part]
            for r in range(rand):
                part = slice((3 + r) * block, (4 + r) * block)
                out_ref[at[r], :, :dim] = dk[part].astype(BF16)
                out_ref[at[r], :, dim:] = dv[part].astype(BF16)
        tok_ref[:, cols] = gk[0].astype(BF16)
        tov_ref[:, cols] = gv[0].astype(BF16)
        tnk_ref[:, cols] = gk[-1].astype(BF16)
        tnv_ref[:, cols] = gv[-1].astype(BF16)
        for b in range(blocks):
            rows = slice(b * block, (b + 1) * block)
            dk_ref[rows, cols] = gk[b + 1]
            dv_ref[rows, cols] = gv[b + 1]


def collect_kernel(
    blocks, block, dim, heads, count, codes, dk_ref, dv_ref, ak_ref, av_ref, bk_ref, bv_ref,
    in_ref, ok_ref, ov_ref, k_acc, v_acc,
):
    last = slice((blocks - 1) * block, blocks * block)
    k_acc[...] = dk_ref[...]
    v_acc[...] = dv_ref[...]
    k_acc[:block] += ak_ref[...].astype(F32)
    v_acc[:block] += av_ref[...].astype(F32)
    k_acc[last] += bk_ref[...].astype(F32)
    v_acc[last] += bv_ref[...].astype(F32)

    @pl.loop(0, count)
    def _(s):
        code = codes[s]

        @pl.when(code >= 0)
        def _():
            rows = pl.ds(pl.multiple_of(code // heads * block, block), block)
            cols = pl.ds(pl.multiple_of(code % heads * dim, dim), dim)
            k_acc[rows, cols] += in_ref[s, :, :dim].astype(F32)
            v_acc[rows, cols] += in_ref[s, :, dim:].astype(F32)

    ok_ref[...] = k_acc[...].astype(BF16)
    ov_ref[...] = v_acc[...].astype(BF16)


def shifted(value, axis, steps):
    count = lax.axis_size(axis)
    first, last = (max(0, -steps), min(count, count - steps))
    return lax.ppermute(value, axis, [(source, source + steps) for source in range(first, last)])


def local(queries, key_rows, value_rows, out_grad, partner):
    peers = lax.axis_size("seq")
    me = lax.axis_index("seq")
    tokens, width = queries.shape
    blocks, heads, rand = partner.shape
    block = tokens // blocks
    dim = width // heads
    scale = 1.0 / math.sqrt(dim)
    items = blocks * heads * rand
    cap = max(2, (3 * items + 2 * peers - 1) // (2 * peers))
    count = peers * cap
    wanted = partner.reshape(items)
    owner = wanted // blocks
    order = jnp.arange(items, dtype=jnp.int32)
    earlier = (owner[None, :] == owner[:, None]) & (order[None, :] < order[:, None])
    slot = owner * cap + jnp.sum(earlier.astype(jnp.int32), axis=1)
    code = wanted % blocks * heads + order // rand % heads
    hit = slot[None, :] == jnp.arange(count, dtype=jnp.int32)[:, None]
    asked = jnp.sum(jnp.where(hit, code[None, :] + 1, 0), axis=1) - 1
    asked = lax.all_to_all(
        asked.reshape(peers, cap), "seq", split_axis=0, concat_axis=0, tiled=True
    ).reshape(count)
    full = pl.BlockSpec(memory_space=VMEM)
    outgoing = pl.pallas_call(
        functools.partial(gather_kernel, block, dim, heads, cap),
        out_shape=jax.ShapeDtypeStruct((count, block, 2 * dim), BF16),
        grid_spec=pltpu.PrefetchScalarGridSpec(
            num_scalar_prefetch=1,
            grid=(peers,),
            in_specs=[pl.BlockSpec((tokens, width), lambda i, *_: (0, 0))] * 2,
            out_specs=pl.BlockSpec((cap, block, 2 * dim), lambda i, *_: (i, 0, 0)),
        ),
        compiler_params=pltpu.CompilerParams(vmem_limit_bytes=LIMIT),
    )(asked, key_rows, value_rows)
    fetched = lax.all_to_all(
        outgoing.reshape(peers, cap, block, 2 * dim), "seq", split_axis=0, concat_axis=0, tiled=True
    ).reshape(count, block, 2 * dim)
    up = shifted(jnp.stack([key_rows[tokens - block:], value_rows[tokens - block:]]), "seq", 1)
    down = shifted(jnp.stack([key_rows[:block], value_rows[:block]]), "seq", -1)
    edge = jnp.stack([(me > 0), (me < peers - 1)]).astype(jnp.int32)
    step = next(n for n in (4, 3, 2, 1) if heads % n == 0)
    wide = pl.BlockSpec((tokens, step * dim), lambda i, *_: (0, i))
    side = pl.BlockSpec((2, block, step * dim), lambda i, *_: (0, 0, i))
    thin = pl.BlockSpec((block, step * dim), lambda i, *_: (0, i))
    far = pl.BlockSpec((count, block, 2 * dim), lambda i, *_: (0, 0, 0))
    half = jax.ShapeDtypeStruct((block, width), BF16)
    whole = jax.ShapeDtypeStruct((tokens, width), F32)
    dq, dk, dv, tok, tov, tnk, tnv, outbound = pl.pallas_call(
        functools.partial(attend_kernel, blocks, block, dim, heads, rand, step, scale),
        out_shape=[
            jax.ShapeDtypeStruct((tokens, width), BF16), whole, whole, half, half, half, half,
            jax.ShapeDtypeStruct((count, block, 2 * dim), BF16),
        ],
        grid_spec=pltpu.PrefetchScalarGridSpec(
            num_scalar_prefetch=2,
            grid=(heads // step,),
            in_specs=[wide, wide, wide, wide, side, side, far],
            out_specs=[wide, wide, wide, thin, thin, thin, thin, far],
        ),
        compiler_params=pltpu.CompilerParams(vmem_limit_bytes=LIMIT),
    )(slot, edge, queries, key_rows, value_rows, out_grad, up, down, fetched)
    inbound = lax.all_to_all(
        outbound.reshape(peers, cap, block, 2 * dim), "seq", split_axis=0, concat_axis=0, tiled=True
    ).reshape(count, block, 2 * dim)
    below_k, below_v = shifted(tok, "seq", -1), shifted(tov, "seq", -1)
    above_k, above_v = shifted(tnk, "seq", 1), shifted(tnv, "seq", 1)
    rows = jax.ShapeDtypeStruct((tokens, width), BF16)
    smem = pl.BlockSpec(memory_space=pltpu.SMEM)
    k_rows, v_rows = pl.pallas_call(
        functools.partial(collect_kernel, blocks, block, dim, heads, count),
        out_shape=[rows, rows],
        in_specs=[smem] + [full] * 7,
        out_specs=[full, full],
        scratch_shapes=[VMEM((tokens, width), F32), VMEM((tokens, width), F32)],
        compiler_params=pltpu.CompilerParams(vmem_limit_bytes=LIMIT),
    )(asked, dk, dv, above_k, above_v, below_k, below_v, inbound)
    return tuple(
        lax.all_to_all(x, "head", split_axis=0, concat_axis=1, tiled=True)
        for x in (dq, k_rows, v_rows)
    )


def solution(mesh):
    placed = (P("seq", "head"),) * 4 + (P("seq", "head", None),)
    return jax.shard_map(
        local,
        mesh=mesh,
        in_specs=placed,
        out_specs=(P(("seq", "head"), None),) * 3,
        check_vma=False,
    )
```

```python
import functools
import math

import jax
import jax.numpy as jnp
from jax import lax
from jax.experimental import pallas as pl
from jax.experimental.pallas import tpu as pltpu
from jax.sharding import PartitionSpec as P

F32 = jnp.float32
BF16 = jnp.bfloat16
VMEM = pltpu.VMEM
LIMIT = 48 * 1024 * 1024


def dot(a, b, ca, cb):
    return lax.dot_general(a, b, (((ca,), (cb,)), ((), ())), preferred_element_type=F32)


def gather_kernel(block, dim, heads, cap, codes, k_ref, v_ref, o_ref):
    peer = pl.program_id(0)
    for j in range(cap):
        code = jnp.maximum(codes[peer * cap + j], 0)
        rows = pl.ds(pl.multiple_of(code // heads * block, block), block)
        cols = pl.ds(pl.multiple_of(code % heads * dim, dim), dim)
        o_ref[j, :, :dim] = k_ref[rows, cols]
        o_ref[j, :, dim:] = v_ref[rows, cols]


def column(ref, index, cols, blocks, block, up, down):
    inner = [ref[b * block:(b + 1) * block, cols] for b in range(blocks)]
    return [up[index, :, cols]] + inner + [down[index, :, cols]]


def attend_kernel(
    blocks, block, dim, heads, rand, step, scale,
    slots, edge, q_ref, k_ref, v_ref, g_ref, up_ref, down_ref, far_ref,
    p_ref, ds_ref, out_ref,
):
    group = pl.program_id(0)
    units = [(j, b) for j in range(step) for b in range(blocks)]
    at, scores, wgrads, vals, qs, gs = [], [], [], [], [], []
    for j, b in units:
        cols = slice(j * dim, (j + 1) * dim)
        rows = slice(b * block, (b + 1) * block)
        head = group * step + j
        at.append([slots[(b * heads + head) * rand + r] for r in range(rand)])
        ks = column(k_ref, 0, cols, blocks, block, up_ref, down_ref)
        vs = column(v_ref, 1, cols, blocks, block, up_ref, down_ref)
        keys = jnp.concatenate(ks[b:b + 3] + [far_ref[s, :, :dim] for s in at[-1]], axis=0)
        vals.append(jnp.concatenate(vs[b:b + 3] + [far_ref[s, :, dim:] for s in at[-1]], axis=0))
        qs.append(q_ref[rows, cols])
        gs.append(g_ref[rows, cols])
        scores.append(scale * dot(qs[-1], keys, 1, 1))
        wgrads.append(dot(gs[-1], vals[-1], 1, 1))
    place = lax.broadcasted_iota(jnp.int32, scores[0].shape, 1)
    for n, (j, b) in enumerate(units):
        if b == 0:
            scores[n] = jnp.where((place < block) & (edge[0] == 0), -jnp.inf, scores[n])
        if b == blocks - 1:
            off = (place >= 2 * block) & (place < 3 * block) & (edge[1] == 0)
            scores[n] = jnp.where(off, -jnp.inf, scores[n])
    tops = [jnp.max(s, axis=1, keepdims=True) for s in scores]
    es = [jnp.exp(s - t) for s, t in zip(scores, tops)]
    ws = [e * (1.0 / jnp.sum(e, axis=1, keepdims=True)) for e in es]
    ps = [w.astype(BF16) for w in ws]
    outs = [dot(p, v, 1, 0).astype(BF16).astype(F32) for p, v in zip(ps, vals)]
    deltas = [jnp.sum(o * g.astype(F32), axis=1, keepdims=True) for o, g in zip(outs, gs)]
    dss = [(w * (wg - d)).astype(BF16) for w, wg, d in zip(ws, wgrads, deltas)]
    dks = [(scale * dot(ds[:, 3 * block:], q, 0, 0)).astype(BF16) for ds, q in zip(dss, qs)]
    dvs = [dot(p[:, 3 * block:], g, 0, 0).astype(BF16) for p, g in zip(ps, gs)]
    for n, (j, b) in enumerate(units):
        rows = slice(b * block, (b + 1) * block)
        p_ref[j, rows] = ps[n][:, :3 * block]
        ds_ref[j, rows] = dss[n]
        for r in range(rand):
            part = slice(r * block, (r + 1) * block)
            out_ref[at[n][r], :, :dim] = dks[n][part]
            out_ref[at[n][r], :, dim:] = dvs[n][part]


def window_kernel(
    blocks, block, dim, heads, rand, step, scale,
    slots, q_ref, k_ref, g_ref, up_ref, down_ref, far_ref, p_ref, ds_ref,
    dq_ref, dk_ref, dv_ref, tok_ref, tov_ref, tnk_ref, tnv_ref,
):
    group = pl.program_id(0)
    for j in range(step):
        head = group * step + j
        cols = slice(j * dim, (j + 1) * dim)
        ks = column(k_ref, 0, cols, blocks, block, up_ref, down_ref)
        gk = [None] * (blocks + 2)
        gv = [None] * (blocks + 2)
        for b in range(blocks):
            rows = slice(b * block, (b + 1) * block)
            q = q_ref[rows, cols]
            g = g_ref[rows, cols]
            at = [slots[(b * heads + head) * rand + r] for r in range(rand)]
            keys = jnp.concatenate(ks[b:b + 3] + [far_ref[s, :, :dim] for s in at], axis=0)
            ds = ds_ref[j, rows]
            dq_ref[rows, cols] = (scale * dot(ds, keys, 1, 0)).astype(BF16)
            dk = scale * dot(ds[:, :3 * block], q, 0, 0)
            dv = dot(p_ref[j, rows], g, 0, 0)
            for i in range(3):
                part = slice(i * block, (i + 1) * block)
                gk[b + i] = dk[part] if gk[b + i] is None else gk[b + i] + dk[part]
                gv[b + i] = dv[part] if gv[b + i] is None else gv[b + i] + dv[part]
        tok_ref[:, cols] = gk[0].astype(BF16)
        tov_ref[:, cols] = gv[0].astype(BF16)
        tnk_ref[:, cols] = gk[-1].astype(BF16)
        tnv_ref[:, cols] = gv[-1].astype(BF16)
        for b in range(blocks):
            rows = slice(b * block, (b + 1) * block)
            dk_ref[rows, cols] = gk[b + 1]
            dv_ref[rows, cols] = gv[b + 1]


def collect_kernel(
    blocks, block, dim, heads, count, codes, dk_ref, dv_ref, ak_ref, av_ref, bk_ref, bv_ref,
    in_ref, ok_ref, ov_ref, k_acc, v_acc,
):
    last = slice((blocks - 1) * block, blocks * block)
    k_acc[...] = dk_ref[...]
    v_acc[...] = dv_ref[...]
    k_acc[:block] += ak_ref[...].astype(F32)
    v_acc[:block] += av_ref[...].astype(F32)
    k_acc[last] += bk_ref[...].astype(F32)
    v_acc[last] += bv_ref[...].astype(F32)

    @pl.loop(0, count)
    def _(s):
        code = codes[s]

        @pl.when(code >= 0)
        def _():
            rows = pl.ds(pl.multiple_of(code // heads * block, block), block)
            cols = pl.ds(pl.multiple_of(code % heads * dim, dim), dim)
            k_acc[rows, cols] += in_ref[s, :, :dim].astype(F32)
            v_acc[rows, cols] += in_ref[s, :, dim:].astype(F32)

    ok_ref[...] = k_acc[...].astype(BF16)
    ov_ref[...] = v_acc[...].astype(BF16)


def shifted(value, axis, steps):
    count = lax.axis_size(axis)
    first, last = (max(0, -steps), min(count, count - steps))
    return lax.ppermute(value, axis, [(source, source + steps) for source in range(first, last)])


def exchanged(x, axis):
    count = lax.axis_size(axis)
    me = lax.axis_index(axis)
    rows, width = x.shape[0] // count, x.shape[1]
    out = jnp.zeros((rows, count * width), x.dtype)
    for r in range(count):
        piece = lax.dynamic_slice_in_dim(x, (me + r) % count * rows, rows, 0)
        if r:
            piece = lax.ppermute(piece, axis, [(i, (i + r) % count) for i in range(count)])
        out = lax.dynamic_update_slice_in_dim(out, piece, (me - r) % count * width, 1)
    return out


def local(queries, key_rows, value_rows, out_grad, partner):
    peers = lax.axis_size("seq")
    me = lax.axis_index("seq")
    tokens, width = queries.shape
    blocks, heads, rand = partner.shape
    block = tokens // blocks
    dim = width // heads
    scale = 1.0 / math.sqrt(dim)
    items = blocks * heads * rand
    cap = max(2, (3 * items + 2 * peers - 1) // (2 * peers))
    count = peers * cap
    wanted = partner.reshape(items)
    owner = wanted // blocks
    order = jnp.arange(items, dtype=jnp.int32)
    earlier = (owner[None, :] == owner[:, None]) & (order[None, :] < order[:, None])
    slot = owner * cap + jnp.sum(earlier.astype(jnp.int32), axis=1)
    code = wanted % blocks * heads + order // rand % heads
    hit = slot[None, :] == jnp.arange(count, dtype=jnp.int32)[:, None]
    asked = jnp.sum(jnp.where(hit, code[None, :] + 1, 0), axis=1) - 1
    asked = lax.all_to_all(
        asked.reshape(peers, cap), "seq", split_axis=0, concat_axis=0, tiled=True
    ).reshape(count)
    full = pl.BlockSpec(memory_space=VMEM)
    up = shifted(jnp.stack([key_rows[tokens - block:], value_rows[tokens - block:]]), "seq", 1)
    down = shifted(jnp.stack([key_rows[:block], value_rows[:block]]), "seq", -1)
    asked, up, down = lax.optimization_barrier((asked, up, down))
    outgoing = pl.pallas_call(
        functools.partial(gather_kernel, block, dim, heads, cap),
        out_shape=jax.ShapeDtypeStruct((count, block, 2 * dim), BF16),
        grid_spec=pltpu.PrefetchScalarGridSpec(
            num_scalar_prefetch=1,
            grid=(peers,),
            in_specs=[pl.BlockSpec((tokens, width), lambda i, *_: (0, 0))] * 2,
            out_specs=pl.BlockSpec((cap, block, 2 * dim), lambda i, *_: (i, 0, 0)),
        ),
        compiler_params=pltpu.CompilerParams(vmem_limit_bytes=LIMIT),
    )(asked, key_rows, value_rows)
    fetched = lax.all_to_all(
        outgoing.reshape(peers, cap, block, 2 * dim), "seq", split_axis=0, concat_axis=0, tiled=True
    ).reshape(count, block, 2 * dim)
    edge = jnp.stack([(me > 0), (me < peers - 1)]).astype(jnp.int32)
    step = next(n for n in (4, 3, 2, 1) if heads % n == 0)
    wide = pl.BlockSpec((tokens, step * dim), lambda i, *_: (0, i))
    side = pl.BlockSpec((2, block, step * dim), lambda i, *_: (0, 0, i))
    thin = pl.BlockSpec((block, step * dim), lambda i, *_: (0, i))
    far = pl.BlockSpec((count, block, 2 * dim), lambda i, *_: (0, 0, 0))
    half = jax.ShapeDtypeStruct((block, width), BF16)
    whole = jax.ShapeDtypeStruct((tokens, width), F32)
    span = 3 * block
    probs = pl.BlockSpec((step, tokens, span), lambda i, *_: (i, 0, 0))
    grads = pl.BlockSpec((step, tokens, span + rand * block), lambda i, *_: (i, 0, 0))
    work = heads * tokens * (span + rand * block) * dim
    cost = pl.CostEstimate(flops=8 * work, bytes_accessed=16 * 2**20, transcendentals=0)
    p, ds, outbound = pl.pallas_call(
        functools.partial(attend_kernel, blocks, block, dim, heads, rand, step, scale),
        out_shape=[
            jax.ShapeDtypeStruct((heads, tokens, span), BF16),
            jax.ShapeDtypeStruct((heads, tokens, span + rand * block), BF16),
            jax.ShapeDtypeStruct((count, block, 2 * dim), BF16),
        ],
        grid_spec=pltpu.PrefetchScalarGridSpec(
            num_scalar_prefetch=2,
            grid=(heads // step,),
            in_specs=[wide, wide, wide, wide, side, side, far],
            out_specs=[probs, grads, far],
        ),
        compiler_params=pltpu.CompilerParams(vmem_limit_bytes=LIMIT),
        cost_estimate=cost,
    )(slot, edge, queries, key_rows, value_rows, out_grad, up, down, fetched)
    dq, dk, dv, tok, tov, tnk, tnv = pl.pallas_call(
        functools.partial(window_kernel, blocks, block, dim, heads, rand, step, scale),
        out_shape=[
            jax.ShapeDtypeStruct((tokens, width), BF16), whole, whole, half, half, half, half,
        ],
        grid_spec=pltpu.PrefetchScalarGridSpec(
            num_scalar_prefetch=1,
            grid=(heads // step,),
            in_specs=[wide, wide, wide, side, side, far, probs, grads],
            out_specs=[wide, wide, wide, thin, thin, thin, thin],
        ),
        compiler_params=pltpu.CompilerParams(vmem_limit_bytes=LIMIT),
        cost_estimate=cost,
    )(slot, queries, key_rows, out_grad, up, down, fetched, p, ds)
    inbound = lax.all_to_all(
        outbound.reshape(peers, cap, block, 2 * dim), "seq", split_axis=0, concat_axis=0, tiled=True
    ).reshape(count, block, 2 * dim)
    below_k, below_v = shifted(tok, "seq", -1), shifted(tov, "seq", -1)
    above_k, above_v = shifted(tnk, "seq", 1), shifted(tnv, "seq", 1)
    rows = jax.ShapeDtypeStruct((tokens, width), BF16)
    smem = pl.BlockSpec(memory_space=pltpu.SMEM)
    k_rows, v_rows = pl.pallas_call(
        functools.partial(collect_kernel, blocks, block, dim, heads, count),
        out_shape=[rows, rows],
        in_specs=[smem] + [full] * 7,
        out_specs=[full, full],
        scratch_shapes=[VMEM((tokens, width), F32), VMEM((tokens, width), F32)],
        compiler_params=pltpu.CompilerParams(vmem_limit_bytes=LIMIT),
    )(asked, dk, dv, above_k, above_v, below_k, below_v, inbound)
    return exchanged(dq, "head"), exchanged(k_rows, "head"), exchanged(v_rows, "head")


def solution(mesh):
    placed = (P("seq", "head"),) * 4 + (P("seq", "head", None),)
    return jax.shard_map(
        local,
        mesh=mesh,
        in_specs=placed,
        out_specs=(P(("seq", "head"), None),) * 3,
        check_vma=False,
    )
```

```python
import functools
import math

import jax
import jax.numpy as jnp
from jax import lax
from jax.experimental import pallas as pl
from jax.experimental.pallas import tpu as pltpu
from jax.sharding import PartitionSpec as P

F32 = jnp.float32
BF16 = jnp.bfloat16
VMEM = pltpu.VMEM
LIMIT = 48 * 1024 * 1024


def dot(a, b, ca, cb):
    return lax.dot_general(a, b, (((ca,), (cb,)), ((), ())), preferred_element_type=F32)


def gather_kernel(block, dim, heads, cap, codes, k_ref, v_ref, o_ref):
    peer = pl.program_id(0)
    for j in range(cap):
        code = jnp.maximum(codes[peer * cap + j], 0)
        rows = pl.ds(pl.multiple_of(code // heads * block, block), block)
        cols = pl.ds(pl.multiple_of(code % heads * dim, dim), dim)
        o_ref[j, :, :dim] = k_ref[rows, cols]
        o_ref[j, :, dim:] = v_ref[rows, cols]


def column(ref, index, cols, blocks, block, up, down):
    inner = [ref[b * block:(b + 1) * block, cols] for b in range(blocks)]
    return [up[index, :, cols]] + inner + [down[index, :, cols]]


def attend_kernel(
    blocks, block, dim, heads, rand, step, scale,
    slots, edge, q_ref, k_ref, v_ref, g_ref, up_ref, down_ref, far_ref,
    p_ref, ds_ref, outk_ref, outv_ref,
):
    group = pl.program_id(0)
    units = [(j, b) for j in range(step) for b in range(blocks)]
    at, scores, wgrads, vals, qs, gs = [], [], [], [], [], []
    for j, b in units:
        cols = slice(j * dim, (j + 1) * dim)
        rows = slice(b * block, (b + 1) * block)
        head = group * step + j
        at.append([slots[(b * heads + head) * rand + r] for r in range(rand)])
        ks = column(k_ref, 0, cols, blocks, block, up_ref, down_ref)
        vs = column(v_ref, 1, cols, blocks, block, up_ref, down_ref)
        keys = jnp.concatenate(ks[b:b + 3] + [far_ref[s, :, :dim] for s in at[-1]], axis=0)
        vals.append(jnp.concatenate(vs[b:b + 3] + [far_ref[s, :, dim:] for s in at[-1]], axis=0))
        qs.append(q_ref[rows, cols])
        gs.append(g_ref[rows, cols])
        scores.append(scale * dot(qs[-1], keys, 1, 1))
        wgrads.append(dot(gs[-1], vals[-1], 1, 1))
    place = lax.broadcasted_iota(jnp.int32, scores[0].shape, 1)
    for n, (j, b) in enumerate(units):
        if b == 0:
            scores[n] = jnp.where((place < block) & (edge[0] == 0), -jnp.inf, scores[n])
        if b == blocks - 1:
            off = (place >= 2 * block) & (place < 3 * block) & (edge[1] == 0)
            scores[n] = jnp.where(off, -jnp.inf, scores[n])
    tops = [jnp.max(s, axis=1, keepdims=True) for s in scores]
    es = [jnp.exp(s - t) for s, t in zip(scores, tops)]
    ws = [e * (1.0 / jnp.sum(e, axis=1, keepdims=True)) for e in es]
    ps = [w.astype(BF16) for w in ws]
    outs = [dot(p, v, 1, 0).astype(BF16).astype(F32) for p, v in zip(ps, vals)]
    deltas = [jnp.sum(o * g.astype(F32), axis=1, keepdims=True) for o, g in zip(outs, gs)]
    dss = [(w * (wg - d)).astype(BF16) for w, wg, d in zip(ws, wgrads, deltas)]
    dks = [(scale * dot(ds[:, 3 * block:], q, 0, 0)).astype(BF16) for ds, q in zip(dss, qs)]
    dvs = [dot(p[:, 3 * block:], g, 0, 0).astype(BF16) for p, g in zip(ps, gs)]
    for n, (j, b) in enumerate(units):
        rows = slice(b * block, (b + 1) * block)
        p_ref[j, rows] = ps[n][:, :3 * block]
        ds_ref[j, rows] = dss[n]
        for r in range(rand):
            part = slice(r * block, (r + 1) * block)
            outk_ref[at[n][r]] = dks[n][part]
            outv_ref[at[n][r]] = dvs[n][part]


def window_kernel(
    blocks, block, dim, heads, rand, step, scale,
    slots, q_ref, k_ref, g_ref, up_ref, down_ref, far_ref, p_ref, ds_ref,
    dq_ref, dk_ref, dv_ref, tok_ref, tov_ref, tnk_ref, tnv_ref,
):
    group = pl.program_id(0)
    for j in range(step):
        head = group * step + j
        cols = slice(j * dim, (j + 1) * dim)
        ks = column(k_ref, 0, cols, blocks, block, up_ref, down_ref)
        gk = [None] * (blocks + 2)
        gv = [None] * (blocks + 2)
        for b in range(blocks):
            rows = slice(b * block, (b + 1) * block)
            q = q_ref[rows, cols]
            g = g_ref[rows, cols]
            at = [slots[(b * heads + head) * rand + r] for r in range(rand)]
            keys = jnp.concatenate(ks[b:b + 3] + [far_ref[s, :, :dim] for s in at], axis=0)
            ds = ds_ref[j, rows]
            dq_ref[rows, cols] = (scale * dot(ds, keys, 1, 0)).astype(BF16)
            dk = scale * dot(ds[:, :3 * block], q, 0, 0)
            dv = dot(p_ref[j, rows], g, 0, 0)
            for i in range(3):
                part = slice(i * block, (i + 1) * block)
                gk[b + i] = dk[part] if gk[b + i] is None else gk[b + i] + dk[part]
                gv[b + i] = dv[part] if gv[b + i] is None else gv[b + i] + dv[part]
        tok_ref[:, cols] = gk[0].astype(BF16)
        tov_ref[:, cols] = gv[0].astype(BF16)
        tnk_ref[:, cols] = gk[-1].astype(BF16)
        tnv_ref[:, cols] = gv[-1].astype(BF16)
        for b in range(blocks):
            rows = slice(b * block, (b + 1) * block)
            dk_ref[rows, cols] = gk[b + 1]
            dv_ref[rows, cols] = gv[b + 1]


def collect_kernel(
    blocks, block, dim, heads, count, codes, own_ref, above_ref, below_ref, in_ref, out_ref, acc,
):
    last = slice((blocks - 1) * block, blocks * block)
    acc[...] = own_ref[...]
    acc[:block] += above_ref[...].astype(F32)
    acc[last] += below_ref[...].astype(F32)

    @pl.loop(0, count)
    def _(s):
        code = codes[s]

        @pl.when(code >= 0)
        def _():
            rows = pl.ds(pl.multiple_of(code // heads * block, block), block)
            cols = pl.ds(pl.multiple_of(code % heads * dim, dim), dim)
            acc[rows, cols] += in_ref[s].astype(F32)

    out_ref[...] = acc[...].astype(BF16)


def shifted(value, axis, steps):
    count = lax.axis_size(axis)
    first, last = (max(0, -steps), min(count, count - steps))
    return lax.ppermute(value, axis, [(source, source + steps) for source in range(first, last)])


def exchanged(x, axis):
    count = lax.axis_size(axis)
    me = lax.axis_index(axis)
    rows, width = x.shape[0] // count, x.shape[1]
    out = jnp.zeros((rows, count * width), x.dtype)
    for r in range(count):
        piece = lax.dynamic_slice_in_dim(x, (me + r) % count * rows, rows, 0)
        if r:
            piece = lax.ppermute(piece, axis, [(i, (i + r) % count) for i in range(count)])
        out = lax.dynamic_update_slice_in_dim(out, piece, (me - r) % count * width, 1)
    return out


def local(queries, key_rows, value_rows, out_grad, partner):
    peers = lax.axis_size("seq")
    me = lax.axis_index("seq")
    tokens, width = queries.shape
    blocks, heads, rand = partner.shape
    block = tokens // blocks
    dim = width // heads
    scale = 1.0 / math.sqrt(dim)
    items = blocks * heads * rand
    cap = max(2, (3 * items + 2 * peers - 1) // (2 * peers))
    count = peers * cap
    wanted = partner.reshape(items)
    owner = wanted // blocks
    order = jnp.arange(items, dtype=jnp.int32)
    earlier = (owner[None, :] == owner[:, None]) & (order[None, :] < order[:, None])
    slot = owner * cap + jnp.sum(earlier.astype(jnp.int32), axis=1)
    code = wanted % blocks * heads + order // rand % heads
    hit = slot[None, :] == jnp.arange(count, dtype=jnp.int32)[:, None]
    asked = jnp.sum(jnp.where(hit, code[None, :] + 1, 0), axis=1) - 1
    asked = lax.all_to_all(
        asked.reshape(peers, cap), "seq", split_axis=0, concat_axis=0, tiled=True
    ).reshape(count)
    full = pl.BlockSpec(memory_space=VMEM)
    up = shifted(jnp.stack([key_rows[tokens - block:], value_rows[tokens - block:]]), "seq", 1)
    down = shifted(jnp.stack([key_rows[:block], value_rows[:block]]), "seq", -1)
    asked, up, down = lax.optimization_barrier((asked, up, down))
    outgoing = pl.pallas_call(
        functools.partial(gather_kernel, block, dim, heads, cap),
        out_shape=jax.ShapeDtypeStruct((count, block, 2 * dim), BF16),
        grid_spec=pltpu.PrefetchScalarGridSpec(
            num_scalar_prefetch=1,
            grid=(peers,),
            in_specs=[pl.BlockSpec((tokens, width), lambda i, *_: (0, 0))] * 2,
            out_specs=pl.BlockSpec((cap, block, 2 * dim), lambda i, *_: (i, 0, 0)),
        ),
        compiler_params=pltpu.CompilerParams(vmem_limit_bytes=LIMIT),
    )(asked, key_rows, value_rows)
    fetched = lax.all_to_all(
        outgoing.reshape(peers, cap, block, 2 * dim), "seq", split_axis=0, concat_axis=0, tiled=True
    ).reshape(count, block, 2 * dim)
    edge = jnp.stack([(me > 0), (me < peers - 1)]).astype(jnp.int32)
    step = next(n for n in (4, 3, 2, 1) if heads % n == 0)
    wide = pl.BlockSpec((tokens, step * dim), lambda i, *_: (0, i))
    side = pl.BlockSpec((2, block, step * dim), lambda i, *_: (0, 0, i))
    thin = pl.BlockSpec((block, step * dim), lambda i, *_: (0, i))
    far = pl.BlockSpec((count, block, 2 * dim), lambda i, *_: (0, 0, 0))
    half = jax.ShapeDtypeStruct((block, width), BF16)
    whole = jax.ShapeDtypeStruct((tokens, width), F32)
    span = 3 * block
    back = pl.BlockSpec((count, block, dim), lambda i, *_: (0, 0, 0))
    probs = pl.BlockSpec((step, tokens, span), lambda i, *_: (i, 0, 0))
    grads = pl.BlockSpec((step, tokens, span + rand * block), lambda i, *_: (i, 0, 0))
    work = heads * tokens * (span + rand * block) * dim
    cost = pl.CostEstimate(flops=8 * work, bytes_accessed=16 * 2**20, transcendentals=0)
    p, ds, outk, outv = pl.pallas_call(
        functools.partial(attend_kernel, blocks, block, dim, heads, rand, step, scale),
        out_shape=[
            jax.ShapeDtypeStruct((heads, tokens, span), BF16),
            jax.ShapeDtypeStruct((heads, tokens, span + rand * block), BF16),
            jax.ShapeDtypeStruct((count, block, dim), BF16),
            jax.ShapeDtypeStruct((count, block, dim), BF16),
        ],
        grid_spec=pltpu.PrefetchScalarGridSpec(
            num_scalar_prefetch=2,
            grid=(heads // step,),
            in_specs=[wide, wide, wide, wide, side, side, far],
            out_specs=[probs, grads, back, back],
        ),
        compiler_params=pltpu.CompilerParams(vmem_limit_bytes=LIMIT),
        cost_estimate=cost,
    )(slot, edge, queries, key_rows, value_rows, out_grad, up, down, fetched)
    dq, dk, dv, tok, tov, tnk, tnv = pl.pallas_call(
        functools.partial(window_kernel, blocks, block, dim, heads, rand, step, scale),
        out_shape=[
            jax.ShapeDtypeStruct((tokens, width), BF16), whole, whole, half, half, half, half,
        ],
        grid_spec=pltpu.PrefetchScalarGridSpec(
            num_scalar_prefetch=1,
            grid=(heads // step,),
            in_specs=[wide, wide, wide, side, side, far, probs, grads],
            out_specs=[wide, wide, wide, thin, thin, thin, thin],
        ),
        compiler_params=pltpu.CompilerParams(vmem_limit_bytes=LIMIT),
        cost_estimate=cost,
    )(slot, queries, key_rows, out_grad, up, down, fetched, p, ds)
    smem = pl.BlockSpec(memory_space=pltpu.SMEM)

    def returned(terms):
        return lax.all_to_all(
            terms.reshape(peers, cap, block, dim), "seq", split_axis=0, concat_axis=0, tiled=True
        ).reshape(count, block, dim)

    def collected(own, above, below, terms):
        return pl.pallas_call(
            functools.partial(collect_kernel, blocks, block, dim, heads, count),
            out_shape=jax.ShapeDtypeStruct((tokens, width), BF16),
            in_specs=[smem] + [full] * 4,
            out_specs=full,
            scratch_shapes=[VMEM((tokens, width), F32)],
            compiler_params=pltpu.CompilerParams(vmem_limit_bytes=LIMIT),
            cost_estimate=pl.CostEstimate(
                flops=0, bytes_accessed=8 * 2**20, transcendentals=0
            ),
        )(asked, own, above, below, terms)

    back_v = returned(outv)
    above_v, below_v = shifted(tnv, "seq", 1), shifted(tov, "seq", -1)
    above_k, below_k = shifted(tnk, "seq", 1), shifted(tok, "seq", -1)
    (outk, back_v) = lax.optimization_barrier((outk, back_v))
    back_k = returned(outk)
    v_rows = collected(dv, above_v, below_v, back_v)
    k_rows = collected(dk, above_k, below_k, back_k)
    return exchanged(dq, "head"), exchanged(k_rows, "head"), exchanged(v_rows, "head")


def solution(mesh):
    placed = (P("seq", "head"),) * 4 + (P("seq", "head", None),)
    return jax.shard_map(
        local,
        mesh=mesh,
        in_specs=placed,
        out_specs=(P(("seq", "head"), None),) * 3,
        check_vma=False,
    )
```

```python
import functools
import math

import jax
import jax.numpy as jnp
from jax import lax
from jax.experimental import pallas as pl
from jax.experimental.pallas import tpu as pltpu
from jax.sharding import PartitionSpec as P

F32 = jnp.float32
BF16 = jnp.bfloat16
VMEM = pltpu.VMEM
LIMIT = 48 * 1024 * 1024


def dot(a, b, ca, cb):
    return lax.dot_general(a, b, (((ca,), (cb,)), ((), ())), preferred_element_type=F32)


def gather_kernel(block, dim, heads, cap, codes, k_ref, v_ref, o_ref):
    peer = pl.program_id(0)
    for j in range(cap):
        code = jnp.maximum(codes[peer * cap + j], 0)
        rows = pl.ds(pl.multiple_of(code // heads * block, block), block)
        cols = pl.ds(pl.multiple_of(code % heads * dim, dim), dim)
        o_ref[j, :, :dim] = k_ref[rows, cols]
        o_ref[j, :, dim:] = v_ref[rows, cols]


def column(ref, index, cols, blocks, block, up, down):
    inner = [ref[b * block:(b + 1) * block, cols] for b in range(blocks)]
    return [up[index, :, cols]] + inner + [down[index, :, cols]]


def attend_kernel(
    blocks, block, dim, heads, rand, step, scale,
    slots, edge, q_ref, k_ref, v_ref, g_ref, up_ref, down_ref, far_ref,
    p_ref, ds_ref, out_ref,
):
    group = pl.program_id(0)
    units = [(j, b) for j in range(step) for b in range(blocks)]
    at, scores, wgrads, vals, qs, gs = [], [], [], [], [], []
    for j, b in units:
        cols = slice(j * dim, (j + 1) * dim)
        rows = slice(b * block, (b + 1) * block)
        head = group * step + j
        at.append([slots[(b * heads + head) * rand + r] for r in range(rand)])
        ks = column(k_ref, 0, cols, blocks, block, up_ref, down_ref)
        vs = column(v_ref, 1, cols, blocks, block, up_ref, down_ref)
        keys = jnp.concatenate(ks[b:b + 3] + [far_ref[s, :, :dim] for s in at[-1]], axis=0)
        vals.append(jnp.concatenate(vs[b:b + 3] + [far_ref[s, :, dim:] for s in at[-1]], axis=0))
        qs.append(q_ref[rows, cols])
        gs.append(g_ref[rows, cols])
        scores.append(scale * dot(qs[-1], keys, 1, 1))
        wgrads.append(dot(gs[-1], vals[-1], 1, 1))
    place = lax.broadcasted_iota(jnp.int32, scores[0].shape, 1)
    for n, (j, b) in enumerate(units):
        if b == 0:
            scores[n] = jnp.where((place < block) & (edge[0] == 0), -jnp.inf, scores[n])
        if b == blocks - 1:
            off = (place >= 2 * block) & (place < 3 * block) & (edge[1] == 0)
            scores[n] = jnp.where(off, -jnp.inf, scores[n])
    tops = [jnp.max(s, axis=1, keepdims=True) for s in scores]
    es = [jnp.exp(s - t) for s, t in zip(scores, tops)]
    ws = [e * (1.0 / jnp.sum(e, axis=1, keepdims=True)) for e in es]
    ps = [w.astype(BF16) for w in ws]
    outs = [dot(p, v, 1, 0).astype(BF16).astype(F32) for p, v in zip(ps, vals)]
    deltas = [jnp.sum(o * g.astype(F32), axis=1, keepdims=True) for o, g in zip(outs, gs)]
    dss = [(w * (wg - d)).astype(BF16) for w, wg, d in zip(ws, wgrads, deltas)]
    dks = [(scale * dot(ds[:, 3 * block:], q, 0, 0)).astype(BF16) for ds, q in zip(dss, qs)]
    dvs = [dot(p[:, 3 * block:], g, 0, 0).astype(BF16) for p, g in zip(ps, gs)]
    for n, (j, b) in enumerate(units):
        rows = slice(b * block, (b + 1) * block)
        p_ref[j, rows] = ps[n][:, :3 * block]
        ds_ref[j, rows] = dss[n]
        for r in range(rand):
            part = slice(r * block, (r + 1) * block)
            out_ref[at[n][r], :, :dim] = dks[n][part]
            out_ref[at[n][r], :, dim:] = dvs[n][part]


def window_kernel(
    blocks, block, dim, heads, rand, step, scale,
    slots, q_ref, k_ref, g_ref, up_ref, down_ref, far_ref, p_ref, ds_ref,
    dq_ref, dk_ref, dv_ref, tok_ref, tov_ref, tnk_ref, tnv_ref,
):
    group = pl.program_id(0)
    for j in range(step):
        head = group * step + j
        cols = slice(j * dim, (j + 1) * dim)
        ks = column(k_ref, 0, cols, blocks, block, up_ref, down_ref)
        gk = [None] * (blocks + 2)
        gv = [None] * (blocks + 2)
        for b in range(blocks):
            rows = slice(b * block, (b + 1) * block)
            q = q_ref[rows, cols]
            g = g_ref[rows, cols]
            at = [slots[(b * heads + head) * rand + r] for r in range(rand)]
            keys = jnp.concatenate(ks[b:b + 3] + [far_ref[s, :, :dim] for s in at], axis=0)
            ds = ds_ref[j, rows]
            dq_ref[rows, cols] = (scale * dot(ds, keys, 1, 0)).astype(BF16)
            dk = scale * dot(ds[:, :3 * block], q, 0, 0)
            dv = dot(p_ref[j, rows], g, 0, 0)
            for i in range(3):
                part = slice(i * block, (i + 1) * block)
                gk[b + i] = dk[part] if gk[b + i] is None else gk[b + i] + dk[part]
                gv[b + i] = dv[part] if gv[b + i] is None else gv[b + i] + dv[part]
        tok_ref[:, cols] = gk[0].astype(BF16)
        tov_ref[:, cols] = gv[0].astype(BF16)
        tnk_ref[:, cols] = gk[-1].astype(BF16)
        tnv_ref[:, cols] = gv[-1].astype(BF16)
        for b in range(blocks):
            rows = slice(b * block, (b + 1) * block)
            dk_ref[rows, cols] = gk[b + 1]
            dv_ref[rows, cols] = gv[b + 1]


def collect_kernel(
    blocks, block, dim, heads, count, first, codes, own_ref, above_ref, below_ref, in_ref, out_ref, acc,
):
    last = slice((blocks - 1) * block, blocks * block)
    acc[...] = own_ref[...]
    acc[:block] += above_ref[...].astype(F32)
    acc[last] += below_ref[...].astype(F32)

    @pl.loop(0, count)
    def _(s):
        code = codes[s]

        @pl.when(code >= 0)
        def _():
            rows = pl.ds(pl.multiple_of(code // heads * block, block), block)
            cols = pl.ds(pl.multiple_of(code % heads * dim, dim), dim)
            acc[rows, cols] += in_ref[s, :, first:first + dim].astype(F32)

    out_ref[...] = acc[...].astype(BF16)


def shifted(value, axis, steps):
    count = lax.axis_size(axis)
    first, last = (max(0, -steps), min(count, count - steps))
    return lax.ppermute(value, axis, [(source, source + steps) for source in range(first, last)])


def exchanged(x, axis):
    count = lax.axis_size(axis)
    me = lax.axis_index(axis)
    rows, width = x.shape[0] // count, x.shape[1]
    out = jnp.zeros((rows, count * width), x.dtype)
    for r in range(count):
        piece = lax.dynamic_slice_in_dim(x, (me + r) % count * rows, rows, 0)
        if r:
            piece = lax.ppermute(piece, axis, [(i, (i + r) % count) for i in range(count)])
        out = lax.dynamic_update_slice_in_dim(out, piece, (me - r) % count * width, 1)
    return out


def local(queries, key_rows, value_rows, out_grad, partner):
    peers = lax.axis_size("seq")
    me = lax.axis_index("seq")
    tokens, width = queries.shape
    blocks, heads, rand = partner.shape
    block = tokens // blocks
    dim = width // heads
    scale = 1.0 / math.sqrt(dim)
    items = blocks * heads * rand
    cap = max(2, (3 * items + 2 * peers - 1) // (2 * peers))
    count = peers * cap
    wanted = partner.reshape(items)
    owner = wanted // blocks
    order = jnp.arange(items, dtype=jnp.int32)
    earlier = (owner[None, :] == owner[:, None]) & (order[None, :] < order[:, None])
    slot = owner * cap + jnp.sum(earlier.astype(jnp.int32), axis=1)
    code = wanted % blocks * heads + order // rand % heads
    hit = slot[None, :] == jnp.arange(count, dtype=jnp.int32)[:, None]
    asked = jnp.sum(jnp.where(hit, code[None, :] + 1, 0), axis=1) - 1
    asked = lax.all_to_all(
        asked.reshape(peers, cap), "seq", split_axis=0, concat_axis=0, tiled=True
    ).reshape(count)
    asked, own_k, own_v = lax.optimization_barrier((asked, key_rows, value_rows))
    up = shifted(jnp.stack([own_k[tokens - block:], own_v[tokens - block:]]), "seq", 1)
    down = shifted(jnp.stack([own_k[:block], own_v[:block]]), "seq", -1)
    full = pl.BlockSpec(memory_space=VMEM)
    outgoing = pl.pallas_call(
        functools.partial(gather_kernel, block, dim, heads, cap),
        out_shape=jax.ShapeDtypeStruct((count, block, 2 * dim), BF16),
        grid_spec=pltpu.PrefetchScalarGridSpec(
            num_scalar_prefetch=1,
            grid=(peers,),
            in_specs=[pl.BlockSpec((tokens, width), lambda i, *_: (0, 0))] * 2,
            out_specs=pl.BlockSpec((cap, block, 2 * dim), lambda i, *_: (i, 0, 0)),
        ),
        compiler_params=pltpu.CompilerParams(vmem_limit_bytes=LIMIT),
        cost_estimate=pl.CostEstimate(flops=0, bytes_accessed=16 * 2**20, transcendentals=0),
    )(asked, own_k, own_v)
    outgoing, up, down = lax.optimization_barrier((outgoing, up, down))
    fetched = lax.all_to_all(
        outgoing.reshape(peers, cap, block, 2 * dim), "seq", split_axis=0, concat_axis=0, tiled=True
    ).reshape(count, block, 2 * dim)
    edge = jnp.stack([(me > 0), (me < peers - 1)]).astype(jnp.int32)
    step = next(n for n in (4, 3, 2, 1) if heads % n == 0)
    wide = pl.BlockSpec((tokens, step * dim), lambda i, *_: (0, i))
    side = pl.BlockSpec((2, block, step * dim), lambda i, *_: (0, 0, i))
    thin = pl.BlockSpec((block, step * dim), lambda i, *_: (0, i))
    far = pl.BlockSpec((count, block, 2 * dim), lambda i, *_: (0, 0, 0))
    half = jax.ShapeDtypeStruct((block, width), BF16)
    whole = jax.ShapeDtypeStruct((tokens, width), F32)
    span = 3 * block
    probs = pl.BlockSpec((step, tokens, span), lambda i, *_: (i, 0, 0))
    grads = pl.BlockSpec((step, tokens, span + rand * block), lambda i, *_: (i, 0, 0))
    work = heads * tokens * (span + rand * block) * dim
    cost = pl.CostEstimate(flops=8 * work, bytes_accessed=16 * 2**20, transcendentals=0)
    p, ds, outbound = pl.pallas_call(
        functools.partial(attend_kernel, blocks, block, dim, heads, rand, step, scale),
        out_shape=[
            jax.ShapeDtypeStruct((heads, tokens, span), BF16),
            jax.ShapeDtypeStruct((heads, tokens, span + rand * block), BF16),
            jax.ShapeDtypeStruct((count, block, 2 * dim), BF16),
        ],
        grid_spec=pltpu.PrefetchScalarGridSpec(
            num_scalar_prefetch=2,
            grid=(heads // step,),
            in_specs=[wide, wide, wide, wide, side, side, far],
            out_specs=[probs, grads, far],
        ),
        compiler_params=pltpu.CompilerParams(vmem_limit_bytes=LIMIT),
        cost_estimate=cost,
    )(slot, edge, queries, key_rows, value_rows, out_grad, up, down, fetched)
    dq, dk, dv, tok, tov, tnk, tnv = pl.pallas_call(
        functools.partial(window_kernel, blocks, block, dim, heads, rand, step, scale),
        out_shape=[
            jax.ShapeDtypeStruct((tokens, width), BF16), whole, whole, half, half, half, half,
        ],
        grid_spec=pltpu.PrefetchScalarGridSpec(
            num_scalar_prefetch=1,
            grid=(heads // step,),
            in_specs=[wide, wide, wide, side, side, far, probs, grads],
            out_specs=[wide, wide, wide, thin, thin, thin, thin],
        ),
        compiler_params=pltpu.CompilerParams(vmem_limit_bytes=LIMIT),
        cost_estimate=cost,
    )(slot, queries, key_rows, out_grad, up, down, fetched, p, ds)
    inbound = lax.all_to_all(
        outbound.reshape(peers, cap, block, 2 * dim), "seq", split_axis=0, concat_axis=0, tiled=True
    ).reshape(count, block, 2 * dim)
    smem = pl.BlockSpec(memory_space=pltpu.SMEM)

    def collected(own, above, below, first):
        return pl.pallas_call(
            functools.partial(collect_kernel, blocks, block, dim, heads, count, first),
            out_shape=jax.ShapeDtypeStruct((tokens, width), BF16),
            in_specs=[smem] + [full] * 4,
            out_specs=full,
            scratch_shapes=[VMEM((tokens, width), F32)],
            compiler_params=pltpu.CompilerParams(vmem_limit_bytes=LIMIT),
            cost_estimate=pl.CostEstimate(
                flops=0, bytes_accessed=8 * 2**20, transcendentals=0
            ),
        )(asked, own, shifted(above, "seq", 1), shifted(below, "seq", -1), inbound)

    k_rows = collected(dk, tnk, tok, 0)
    v_rows = collected(dv, tnv, tov, dim)
    return exchanged(dq, "head"), exchanged(k_rows, "head"), exchanged(v_rows, "head")


def solution(mesh):
    placed = (P("seq", "head"),) * 4 + (P("seq", "head", None),)
    return jax.shard_map(
        local,
        mesh=mesh,
        in_specs=placed,
        out_specs=(P(("seq", "head"), None),) * 3,
        check_vma=False,
    )
```

```python
import functools
import math

import jax
import jax.numpy as jnp
from jax import lax
from jax.experimental import pallas as pl
from jax.experimental.pallas import tpu as pltpu
from jax.sharding import PartitionSpec as P

F32 = jnp.float32
BF16 = jnp.bfloat16
VMEM = pltpu.VMEM
LIMIT = 48 * 1024 * 1024


def dot(a, b, ca, cb):
    return lax.dot_general(a, b, (((ca,), (cb,)), ((), ())), preferred_element_type=F32)


def gather_kernel(block, dim, heads, cap, codes, k_ref, v_ref, o_ref):
    peer = pl.program_id(0)
    for j in range(cap):
        code = jnp.maximum(codes[peer * cap + j], 0)
        rows = pl.ds(pl.multiple_of(code // heads * block, block), block)
        cols = pl.ds(pl.multiple_of(code % heads * dim, dim), dim)
        o_ref[j, :, :dim] = k_ref[rows, cols]
        o_ref[j, :, dim:] = v_ref[rows, cols]


def column(ref, index, cols, blocks, block, up, down):
    inner = [ref[b * block:(b + 1) * block, cols] for b in range(blocks)]
    return [up[index, :, cols]] + inner + [down[index, :, cols]]


def attend_kernel(
    blocks, block, dim, heads, rand, step, scale,
    slots, edge, q_ref, k_ref, v_ref, g_ref, up_ref, down_ref, far_ref,
    p_ref, ds_ref, out_ref,
):
    group = pl.program_id(0)
    units = [(j, b) for j in range(step) for b in range(blocks)]
    at, scores, wgrads, vals, qs, gs = [], [], [], [], [], []
    for j, b in units:
        cols = slice(j * dim, (j + 1) * dim)
        rows = slice(b * block, (b + 1) * block)
        head = group * step + j
        at.append([slots[(b * heads + head) * rand + r] for r in range(rand)])
        ks = column(k_ref, 0, cols, blocks, block, up_ref, down_ref)
        vs = column(v_ref, 1, cols, blocks, block, up_ref, down_ref)
        keys = jnp.concatenate(ks[b:b + 3] + [far_ref[s, :, :dim] for s in at[-1]], axis=0)
        vals.append(jnp.concatenate(vs[b:b + 3] + [far_ref[s, :, dim:] for s in at[-1]], axis=0))
        qs.append(q_ref[rows, cols])
        gs.append(g_ref[rows, cols])
        scores.append(scale * dot(qs[-1], keys, 1, 1))
        wgrads.append(dot(gs[-1], vals[-1], 1, 1))
    place = lax.broadcasted_iota(jnp.int32, scores[0].shape, 1)
    for n, (j, b) in enumerate(units):
        if b == 0:
            scores[n] = jnp.where((place < block) & (edge[0] == 0), -jnp.inf, scores[n])
        if b == blocks - 1:
            off = (place >= 2 * block) & (place < 3 * block) & (edge[1] == 0)
            scores[n] = jnp.where(off, -jnp.inf, scores[n])
    tops = [jnp.max(s, axis=1, keepdims=True) for s in scores]
    es = [jnp.exp(s - t) for s, t in zip(scores, tops)]
    ws = [e * (1.0 / jnp.sum(e, axis=1, keepdims=True)) for e in es]
    ps = [w.astype(BF16) for w in ws]
    outs = [dot(p, v, 1, 0).astype(BF16).astype(F32) for p, v in zip(ps, vals)]
    deltas = [jnp.sum(o * g.astype(F32), axis=1, keepdims=True) for o, g in zip(outs, gs)]
    dss = [(w * (wg - d)).astype(BF16) for w, wg, d in zip(ws, wgrads, deltas)]
    dks = [(scale * dot(ds[:, 3 * block:], q, 0, 0)).astype(BF16) for ds, q in zip(dss, qs)]
    dvs = [dot(p[:, 3 * block:], g, 0, 0).astype(BF16) for p, g in zip(ps, gs)]
    for n, (j, b) in enumerate(units):
        rows = slice(b * block, (b + 1) * block)
        p_ref[j, rows] = ps[n][:, :3 * block]
        ds_ref[j, rows] = dss[n]
        for r in range(rand):
            part = slice(r * block, (r + 1) * block)
            out_ref[at[n][r], :, :dim] = dks[n][part]
            out_ref[at[n][r], :, dim:] = dvs[n][part]


def window_kernel(
    blocks, block, dim, heads, rand, step, scale,
    slots, q_ref, k_ref, g_ref, up_ref, down_ref, far_ref, p_ref, ds_ref,
    dq_ref, dk_ref, dv_ref, tok_ref, tov_ref, tnk_ref, tnv_ref,
):
    group = pl.program_id(0)
    for j in range(step):
        head = group * step + j
        cols = slice(j * dim, (j + 1) * dim)
        ks = column(k_ref, 0, cols, blocks, block, up_ref, down_ref)
        gk = [None] * (blocks + 2)
        gv = [None] * (blocks + 2)
        for b in range(blocks):
            rows = slice(b * block, (b + 1) * block)
            q = q_ref[rows, cols]
            g = g_ref[rows, cols]
            at = [slots[(b * heads + head) * rand + r] for r in range(rand)]
            keys = jnp.concatenate(ks[b:b + 3] + [far_ref[s, :, :dim] for s in at], axis=0)
            ds = ds_ref[j, rows]
            dq_ref[rows, cols] = (scale * dot(ds, keys, 1, 0)).astype(BF16)
            dk = scale * dot(ds[:, :3 * block], q, 0, 0)
            dv = dot(p_ref[j, rows], g, 0, 0)
            for i in range(3):
                part = slice(i * block, (i + 1) * block)
                gk[b + i] = dk[part] if gk[b + i] is None else gk[b + i] + dk[part]
                gv[b + i] = dv[part] if gv[b + i] is None else gv[b + i] + dv[part]
        tok_ref[:, cols] = gk[0].astype(BF16)
        tov_ref[:, cols] = gv[0].astype(BF16)
        tnk_ref[:, cols] = gk[-1].astype(BF16)
        tnv_ref[:, cols] = gv[-1].astype(BF16)
        for b in range(blocks):
            rows = slice(b * block, (b + 1) * block)
            dk_ref[rows, cols] = gk[b + 1]
            dv_ref[rows, cols] = gv[b + 1]


def collect_kernel(
    blocks, block, dim, heads, count, first, codes, own_ref, above_ref, below_ref, in_ref, out_ref, acc,
):
    last = slice((blocks - 1) * block, blocks * block)
    acc[...] = own_ref[...]
    acc[:block] += above_ref[...].astype(F32)
    acc[last] += below_ref[...].astype(F32)

    batch = next(n for n in (8, 4, 2, 1) if count % n == 0)

    @pl.loop(0, count // batch)
    def _(i):
        for j in range(batch):
            code = codes[i * batch + j]
            term = in_ref[i * batch + j, :, first:first + dim].astype(F32)
            term = jnp.where(code >= 0, term, 0.0)
            code = jnp.maximum(code, 0)
            rows = pl.ds(pl.multiple_of(code // heads * block, block), block)
            cols = pl.ds(pl.multiple_of(code % heads * dim, dim), dim)
            acc[rows, cols] += term

    out_ref[...] = acc[...].astype(BF16)


def shifted(value, axis, steps):
    count = lax.axis_size(axis)
    first, last = (max(0, -steps), min(count, count - steps))
    return lax.ppermute(value, axis, [(source, source + steps) for source in range(first, last)])


def exchanged(x, axis):
    count = lax.axis_size(axis)
    me = lax.axis_index(axis)
    rows, width = x.shape[0] // count, x.shape[1]
    out = jnp.zeros((rows, count * width), x.dtype)
    for r in range(count):
        piece = lax.dynamic_slice_in_dim(x, (me + r) % count * rows, rows, 0)
        if r:
            piece = lax.ppermute(piece, axis, [(i, (i + r) % count) for i in range(count)])
        out = lax.dynamic_update_slice_in_dim(out, piece, (me - r) % count * width, 1)
    return out


def local(queries, key_rows, value_rows, out_grad, partner):
    peers = lax.axis_size("seq")
    me = lax.axis_index("seq")
    tokens, width = queries.shape
    blocks, heads, rand = partner.shape
    block = tokens // blocks
    dim = width // heads
    scale = 1.0 / math.sqrt(dim)
    items = blocks * heads * rand
    cap = max(2, (3 * items + 2 * peers - 1) // (2 * peers))
    count = peers * cap
    wanted = partner.reshape(items)
    owner = wanted // blocks
    order = jnp.arange(items, dtype=jnp.int32)
    earlier = (owner[None, :] == owner[:, None]) & (order[None, :] < order[:, None])
    slot = owner * cap + jnp.sum(earlier.astype(jnp.int32), axis=1)
    code = wanted % blocks * heads + order // rand % heads
    hit = slot[None, :] == jnp.arange(count, dtype=jnp.int32)[:, None]
    asked = jnp.sum(jnp.where(hit, code[None, :] + 1, 0), axis=1) - 1
    asked = lax.all_to_all(
        asked.reshape(peers, cap), "seq", split_axis=0, concat_axis=0, tiled=True
    ).reshape(count)
    asked, own_k, own_v = lax.optimization_barrier((asked, key_rows, value_rows))
    up = shifted(jnp.stack([own_k[tokens - block:], own_v[tokens - block:]]), "seq", 1)
    down = shifted(jnp.stack([own_k[:block], own_v[:block]]), "seq", -1)
    full = pl.BlockSpec(memory_space=VMEM)
    up = shifted(jnp.stack([key_rows[tokens - block:], value_rows[tokens - block:]]), "seq", 1)
    down = shifted(jnp.stack([key_rows[:block], value_rows[:block]]), "seq", -1)
    asked, up, down = lax.optimization_barrier((asked, up, down))
    outgoing = pl.pallas_call(
        functools.partial(gather_kernel, block, dim, heads, cap),
        out_shape=jax.ShapeDtypeStruct((count, block, 2 * dim), BF16),
        grid_spec=pltpu.PrefetchScalarGridSpec(
            num_scalar_prefetch=1,
            grid=(peers,),
            in_specs=[pl.BlockSpec((tokens, width), lambda i, *_: (0, 0))] * 2,
            out_specs=pl.BlockSpec((cap, block, 2 * dim), lambda i, *_: (i, 0, 0)),
        ),
        compiler_params=pltpu.CompilerParams(vmem_limit_bytes=LIMIT),
    )(asked, key_rows, value_rows)
    fetched = lax.all_to_all(
        outgoing.reshape(peers, cap, block, 2 * dim), "seq", split_axis=0, concat_axis=0, tiled=True
    ).reshape(count, block, 2 * dim)
    edge = jnp.stack([(me > 0), (me < peers - 1)]).astype(jnp.int32)
    step = next(n for n in (4, 3, 2, 1) if heads % n == 0)
    wide = pl.BlockSpec((tokens, step * dim), lambda i, *_: (0, i))
    side = pl.BlockSpec((2, block, step * dim), lambda i, *_: (0, 0, i))
    thin = pl.BlockSpec((block, step * dim), lambda i, *_: (0, i))
    far = pl.BlockSpec((count, block, 2 * dim), lambda i, *_: (0, 0, 0))
    half = jax.ShapeDtypeStruct((block, width), BF16)
    whole = jax.ShapeDtypeStruct((tokens, width), F32)
    span = 3 * block
    probs = pl.BlockSpec((step, tokens, span), lambda i, *_: (i, 0, 0))
    grads = pl.BlockSpec((step, tokens, span + rand * block), lambda i, *_: (i, 0, 0))
    work = heads * tokens * (span + rand * block) * dim
    cost = pl.CostEstimate(flops=8 * work, bytes_accessed=16 * 2**20, transcendentals=0)
    p, ds, outbound = pl.pallas_call(
        functools.partial(attend_kernel, blocks, block, dim, heads, rand, step, scale),
        out_shape=[
            jax.ShapeDtypeStruct((heads, tokens, span), BF16),
            jax.ShapeDtypeStruct((heads, tokens, span + rand * block), BF16),
            jax.ShapeDtypeStruct((count, block, 2 * dim), BF16),
        ],
        grid_spec=pltpu.PrefetchScalarGridSpec(
            num_scalar_prefetch=2,
            grid=(heads // step,),
            in_specs=[wide, wide, wide, wide, side, side, far],
            out_specs=[probs, grads, far],
        ),
        compiler_params=pltpu.CompilerParams(vmem_limit_bytes=LIMIT),
        cost_estimate=cost,
    )(slot, edge, queries, key_rows, value_rows, out_grad, up, down, fetched)
    dq, dk, dv, tok, tov, tnk, tnv = pl.pallas_call(
        functools.partial(window_kernel, blocks, block, dim, heads, rand, step, scale),
        out_shape=[
            jax.ShapeDtypeStruct((tokens, width), BF16), whole, whole, half, half, half, half,
        ],
        grid_spec=pltpu.PrefetchScalarGridSpec(
            num_scalar_prefetch=1,
            grid=(heads // step,),
            in_specs=[wide, wide, wide, side, side, far, probs, grads],
            out_specs=[wide, wide, wide, thin, thin, thin, thin],
        ),
        compiler_params=pltpu.CompilerParams(vmem_limit_bytes=LIMIT),
        cost_estimate=cost,
    )(slot, queries, key_rows, out_grad, up, down, fetched, p, ds)
    inbound = lax.all_to_all(
        outbound.reshape(peers, cap, block, 2 * dim), "seq", split_axis=0, concat_axis=0, tiled=True
    ).reshape(count, block, 2 * dim)
    smem = pl.BlockSpec(memory_space=pltpu.SMEM)

    def collected(own, above, below, first):
        return pl.pallas_call(
            functools.partial(collect_kernel, blocks, block, dim, heads, count, first),
            out_shape=jax.ShapeDtypeStruct((tokens, width), BF16),
            in_specs=[smem] + [full] * 4,
            out_specs=full,
            scratch_shapes=[VMEM((tokens, width), F32)],
            compiler_params=pltpu.CompilerParams(vmem_limit_bytes=LIMIT),
            cost_estimate=pl.CostEstimate(
                flops=0, bytes_accessed=8 * 2**20, transcendentals=0
            ),
        )(asked, own, shifted(above, "seq", 1), shifted(below, "seq", -1), inbound)

    k_rows = collected(dk, tnk, tok, 0)
    v_rows = collected(dv, tnv, tov, dim)
    return exchanged(dq, "head"), exchanged(k_rows, "head"), exchanged(v_rows, "head")


def solution(mesh):
    placed = (P("seq", "head"),) * 4 + (P("seq", "head", None),)
    return jax.shard_map(
        local,
        mesh=mesh,
        in_specs=placed,
        out_specs=(P(("seq", "head"), None),) * 3,
        check_vma=False,
    )
```

```python
import functools
import math

import jax
import jax.numpy as jnp
from jax import lax
from jax.experimental import pallas as pl
from jax.experimental.pallas import tpu as pltpu
from jax.sharding import PartitionSpec as P

F32 = jnp.float32
BF16 = jnp.bfloat16
VMEM = pltpu.VMEM
LIMIT = 48 * 1024 * 1024


def dot(a, b, ca, cb):
    return lax.dot_general(a, b, (((ca,), (cb,)), ((), ())), preferred_element_type=F32)


def gather_kernel(block, dim, heads, cap, codes, k_ref, v_ref, o_ref):
    peer = pl.program_id(0)
    for j in range(cap):
        code = jnp.maximum(codes[peer * cap + j], 0)
        rows = pl.ds(pl.multiple_of(code // heads * block, block), block)
        cols = pl.ds(pl.multiple_of(code % heads * dim, dim), dim)
        o_ref[j, :, :dim] = k_ref[rows, cols]
        o_ref[j, :, dim:] = v_ref[rows, cols]


def column(ref, index, cols, blocks, block, up, down):
    inner = [ref[b * block:(b + 1) * block, cols] for b in range(blocks)]
    return [up[index, :, cols]] + inner + [down[index, :, cols]]


def attend_kernel(
    blocks, block, dim, heads, rand, step, scale,
    slots, edge, q_ref, k_ref, v_ref, g_ref, up_ref, down_ref, far_ref,
    p_ref, ds_ref, out_ref,
):
    group = pl.program_id(0)
    units = [(j, b) for j in range(step) for b in range(blocks)]
    at, scores, wgrads, vals, qs, gs = [], [], [], [], [], []
    for j, b in units:
        cols = slice(j * dim, (j + 1) * dim)
        rows = slice(b * block, (b + 1) * block)
        head = group * step + j
        at.append([slots[(b * heads + head) * rand + r] for r in range(rand)])
        ks = column(k_ref, 0, cols, blocks, block, up_ref, down_ref)
        vs = column(v_ref, 1, cols, blocks, block, up_ref, down_ref)
        keys = jnp.concatenate(ks[b:b + 3] + [far_ref[s, :, :dim] for s in at[-1]], axis=0)
        vals.append(jnp.concatenate(vs[b:b + 3] + [far_ref[s, :, dim:] for s in at[-1]], axis=0))
        qs.append(q_ref[rows, cols])
        gs.append(g_ref[rows, cols])
        scores.append(scale * dot(qs[-1], keys, 1, 1))
        wgrads.append(dot(gs[-1], vals[-1], 1, 1))
    place = lax.broadcasted_iota(jnp.int32, scores[0].shape, 1)
    for n, (j, b) in enumerate(units):
        if b == 0:
            scores[n] = jnp.where((place < block) & (edge[0] == 0), -jnp.inf, scores[n])
        if b == blocks - 1:
            off = (place >= 2 * block) & (place < 3 * block) & (edge[1] == 0)
            scores[n] = jnp.where(off, -jnp.inf, scores[n])
    tops = [jnp.max(s, axis=1, keepdims=True) for s in scores]
    es = [jnp.exp(s - t) for s, t in zip(scores, tops)]
    ws = [e * (1.0 / jnp.sum(e, axis=1, keepdims=True)) for e in es]
    ps = [w.astype(BF16) for w in ws]
    outs = [dot(p, v, 1, 0).astype(BF16).astype(F32) for p, v in zip(ps, vals)]
    deltas = [jnp.sum(o * g.astype(F32), axis=1, keepdims=True) for o, g in zip(outs, gs)]
    dss = [(w * (wg - d)).astype(BF16) for w, wg, d in zip(ws, wgrads, deltas)]
    dks = [(scale * dot(ds[:, 3 * block:], q, 0, 0)).astype(BF16) for ds, q in zip(dss, qs)]
    dvs = [dot(p[:, 3 * block:], g, 0, 0).astype(BF16) for p, g in zip(ps, gs)]
    for n, (j, b) in enumerate(units):
        rows = slice(b * block, (b + 1) * block)
        p_ref[j, rows] = ps[n][:, :3 * block]
        ds_ref[j, rows] = dss[n]
        for r in range(rand):
            part = slice(r * block, (r + 1) * block)
            out_ref[at[n][r], :, :dim] = dks[n][part]
            out_ref[at[n][r], :, dim:] = dvs[n][part]


def window_kernel(
    blocks, block, dim, heads, rand, step, scale,
    slots, q_ref, k_ref, g_ref, up_ref, down_ref, far_ref, p_ref, ds_ref,
    dq_ref, dk_ref, dv_ref, tok_ref, tov_ref, tnk_ref, tnv_ref,
):
    group = pl.program_id(0)
    for j in range(step):
        head = group * step + j
        cols = slice(j * dim, (j + 1) * dim)
        ks = column(k_ref, 0, cols, blocks, block, up_ref, down_ref)
        gk = [None] * (blocks + 2)
        gv = [None] * (blocks + 2)
        for b in range(blocks):
            rows = slice(b * block, (b + 1) * block)
            q = q_ref[rows, cols]
            g = g_ref[rows, cols]
            at = [slots[(b * heads + head) * rand + r] for r in range(rand)]
            keys = jnp.concatenate(ks[b:b + 3] + [far_ref[s, :, :dim] for s in at], axis=0)
            ds = ds_ref[j, rows]
            dq_ref[rows, cols] = (scale * dot(ds, keys, 1, 0)).astype(BF16)
            dk = scale * dot(ds[:, :3 * block], q, 0, 0)
            dv = dot(p_ref[j, rows], g, 0, 0)
            for i in range(3):
                part = slice(i * block, (i + 1) * block)
                gk[b + i] = dk[part] if gk[b + i] is None else gk[b + i] + dk[part]
                gv[b + i] = dv[part] if gv[b + i] is None else gv[b + i] + dv[part]
        tok_ref[:, cols] = gk[0].astype(BF16)
        tov_ref[:, cols] = gv[0].astype(BF16)
        tnk_ref[:, cols] = gk[-1].astype(BF16)
        tnv_ref[:, cols] = gv[-1].astype(BF16)
        for b in range(blocks):
            rows = slice(b * block, (b + 1) * block)
            dk_ref[rows, cols] = gk[b + 1]
            dv_ref[rows, cols] = gv[b + 1]


def collect_kernel(
    blocks, block, dim, heads, count, first, codes, own_ref, above_ref, below_ref, in_ref, out_ref, acc,
):
    last = slice((blocks - 1) * block, blocks * block)
    acc[...] = own_ref[...]
    acc[:block] += above_ref[...].astype(F32)
    acc[last] += below_ref[...].astype(F32)

    batch = next(n for n in (8, 4, 2, 1) if count % n == 0)

    @pl.loop(0, count // batch)
    def _(i):
        for j in range(batch):
            code = codes[i * batch + j]
            term = in_ref[i * batch + j, :, first:first + dim].astype(F32)
            term = jnp.where(code >= 0, term, 0.0)
            code = jnp.maximum(code, 0)
            rows = pl.ds(pl.multiple_of(code // heads * block, block), block)
            cols = pl.ds(pl.multiple_of(code % heads * dim, dim), dim)
            acc[rows, cols] += term

    out_ref[...] = acc[...].astype(BF16)


def shifted(value, axis, steps):
    count = lax.axis_size(axis)
    first, last = (max(0, -steps), min(count, count - steps))
    return lax.ppermute(value, axis, [(source, source + steps) for source in range(first, last)])


def exchanged(x, axis):
    count = lax.axis_size(axis)
    me = lax.axis_index(axis)
    rows, width = x.shape[0] // count, x.shape[1]
    out = jnp.zeros((rows, count * width), x.dtype)
    for r in range(count):
        piece = lax.dynamic_slice_in_dim(x, (me + r) % count * rows, rows, 0)
        if r:
            piece = lax.ppermute(piece, axis, [(i, (i + r) % count) for i in range(count)])
        out = lax.dynamic_update_slice_in_dim(out, piece, (me - r) % count * width, 1)
    return out


def local(queries, key_rows, value_rows, out_grad, partner):
    peers = lax.axis_size("seq")
    me = lax.axis_index("seq")
    tokens, width = queries.shape
    blocks, heads, rand = partner.shape
    block = tokens // blocks
    dim = width // heads
    scale = 1.0 / math.sqrt(dim)
    items = blocks * heads * rand
    cap = max(2, (3 * items + 2 * peers - 1) // (2 * peers))
    count = peers * cap
    wanted = partner.reshape(items)
    owner = wanted // blocks
    order = jnp.arange(items, dtype=jnp.int32)
    earlier = (owner[None, :] == owner[:, None]) & (order[None, :] < order[:, None])
    slot = owner * cap + jnp.sum(earlier.astype(jnp.int32), axis=1)
    code = wanted % blocks * heads + order // rand % heads
    hit = slot[None, :] == jnp.arange(count, dtype=jnp.int32)[:, None]
    asked = jnp.sum(jnp.where(hit, code[None, :] + 1, 0), axis=1) - 1
    asked = lax.all_to_all(
        asked.reshape(peers, cap), "seq", split_axis=0, concat_axis=0, tiled=True
    ).reshape(count)
    asked, own_k, own_v = lax.optimization_barrier((asked, key_rows, value_rows))
    up = shifted(jnp.stack([own_k[tokens - block:], own_v[tokens - block:]]), "seq", 1)
    down = shifted(jnp.stack([own_k[:block], own_v[:block]]), "seq", -1)
    full = pl.BlockSpec(memory_space=VMEM)
    up = shifted(jnp.stack([key_rows[tokens - block:], value_rows[tokens - block:]]), "seq", 1)
    down = shifted(jnp.stack([key_rows[:block], value_rows[:block]]), "seq", -1)
    asked, up, down = lax.optimization_barrier((asked, up, down))
    outgoing = pl.pallas_call(
        functools.partial(gather_kernel, block, dim, heads, cap),
        out_shape=jax.ShapeDtypeStruct((count, block, 2 * dim), BF16),
        grid_spec=pltpu.PrefetchScalarGridSpec(
            num_scalar_prefetch=1,
            grid=(peers,),
            in_specs=[pl.BlockSpec((tokens, width), lambda i, *_: (0, 0))] * 2,
            out_specs=pl.BlockSpec((cap, block, 2 * dim), lambda i, *_: (i, 0, 0)),
        ),
        compiler_params=pltpu.CompilerParams(vmem_limit_bytes=LIMIT),
    )(asked, key_rows, value_rows)
    fetched = lax.all_to_all(
        outgoing.reshape(peers, cap, block, 2 * dim), "seq", split_axis=0, concat_axis=0, tiled=True
    ).reshape(count, block, 2 * dim)
    edge = jnp.stack([(me > 0), (me < peers - 1)]).astype(jnp.int32)
    step = next(n for n in (6, 4, 3, 2, 1) if heads % n == 0)
    wide = pl.BlockSpec((tokens, step * dim), lambda i, *_: (0, i))
    side = pl.BlockSpec((2, block, step * dim), lambda i, *_: (0, 0, i))
    thin = pl.BlockSpec((block, step * dim), lambda i, *_: (0, i))
    far = pl.BlockSpec((count, block, 2 * dim), lambda i, *_: (0, 0, 0))
    half = jax.ShapeDtypeStruct((block, width), BF16)
    whole = jax.ShapeDtypeStruct((tokens, width), F32)
    span = 3 * block
    probs = pl.BlockSpec((step, tokens, span), lambda i, *_: (i, 0, 0))
    grads = pl.BlockSpec((step, tokens, span + rand * block), lambda i, *_: (i, 0, 0))
    work = heads * tokens * (span + rand * block) * dim
    cost = pl.CostEstimate(flops=8 * work, bytes_accessed=16 * 2**20, transcendentals=0)
    p, ds, outbound = pl.pallas_call(
        functools.partial(attend_kernel, blocks, block, dim, heads, rand, step, scale),
        out_shape=[
            jax.ShapeDtypeStruct((heads, tokens, span), BF16),
            jax.ShapeDtypeStruct((heads, tokens, span + rand * block), BF16),
            jax.ShapeDtypeStruct((count, block, 2 * dim), BF16),
        ],
        grid_spec=pltpu.PrefetchScalarGridSpec(
            num_scalar_prefetch=2,
            grid=(heads // step,),
            in_specs=[wide, wide, wide, wide, side, side, far],
            out_specs=[probs, grads, far],
        ),
        compiler_params=pltpu.CompilerParams(vmem_limit_bytes=LIMIT),
        cost_estimate=cost,
    )(slot, edge, queries, key_rows, value_rows, out_grad, up, down, fetched)
    dq, dk, dv, tok, tov, tnk, tnv = pl.pallas_call(
        functools.partial(window_kernel, blocks, block, dim, heads, rand, step, scale),
        out_shape=[
            jax.ShapeDtypeStruct((tokens, width), BF16), whole, whole, half, half, half, half,
        ],
        grid_spec=pltpu.PrefetchScalarGridSpec(
            num_scalar_prefetch=1,
            grid=(heads // step,),
            in_specs=[wide, wide, wide, side, side, far, probs, grads],
            out_specs=[wide, wide, wide, thin, thin, thin, thin],
        ),
        compiler_params=pltpu.CompilerParams(vmem_limit_bytes=LIMIT),
        cost_estimate=cost,
    )(slot, queries, key_rows, out_grad, up, down, fetched, p, ds)
    inbound = lax.all_to_all(
        outbound.reshape(peers, cap, block, 2 * dim), "seq", split_axis=0, concat_axis=0, tiled=True
    ).reshape(count, block, 2 * dim)
    smem = pl.BlockSpec(memory_space=pltpu.SMEM)

    def collected(own, above, below, first):
        return pl.pallas_call(
            functools.partial(collect_kernel, blocks, block, dim, heads, count, first),
            out_shape=jax.ShapeDtypeStruct((tokens, width), BF16),
            in_specs=[smem] + [full] * 4,
            out_specs=full,
            scratch_shapes=[VMEM((tokens, width), F32)],
            compiler_params=pltpu.CompilerParams(vmem_limit_bytes=LIMIT),
            cost_estimate=pl.CostEstimate(
                flops=0, bytes_accessed=8 * 2**20, transcendentals=0
            ),
        )(asked, own, shifted(above, "seq", 1), shifted(below, "seq", -1), inbound)

    k_rows = collected(dk, tnk, tok, 0)
    v_rows = collected(dv, tnv, tov, dim)
    return exchanged(dq, "head"), exchanged(k_rows, "head"), exchanged(v_rows, "head")


def solution(mesh):
    placed = (P("seq", "head"),) * 4 + (P("seq", "head", None),)
    return jax.shard_map(
        local,
        mesh=mesh,
        in_specs=placed,
        out_specs=(P(("seq", "head"), None),) * 3,
        check_vma=False,
    )
```
